256 devices in a mesh: ctx: 64 (over y_hi, x, z), grp: 4 (over y_lo, core).
Axes of the slice: x: 4, y: 4 (y_hi: 2, y_lo: 2; y = y_hi * 2 + y_lo), z: 8, core: 2. Of those that a mesh axis runs over, the one named last changes fastest.
Arguments:
- queries: bfloat16 [32768, 4096], P('ctx', 'grp'), parts along dimension 1, may hold values from -6 to 6
- keys: bfloat16 [32768, 512], P('ctx', 'grp'), parts along dimension 1, may hold values from -6 to 6
- values: bfloat16 [32768, 512], P('ctx', 'grp'), parts along dimension 1, may hold values from -6 to 6
- outputs: bfloat16 [32768, 4096], P('ctx', 'grp'), parts along dimension 1, may hold values from -6 to 6
- out_grad: bfloat16 [32768, 4096], P('ctx', 'grp'), parts along dimension 1, may hold values from -6 to 6
- log_sums: float32 [32, 32768], P('grp', 'ctx'), parts along dimension 0, may hold values from 3 to 6
- pair_of: int32 [64], replicated, may hold values from 0 to 63, each once
Outputs:
- grad_queries: bfloat16 [32768, 4096], P('ctx', 'grp'), parts along dimension 1
- grad_keys: float32 [32768, 512], P('ctx', 'grp'), parts along dimension 1
- grad_values: float32 [32768, 512], P('ctx', 'grp'), parts along dimension 1
The draws below stay inside these ranges and needn't reach their ends.
There are 4 independent parts, one for each index of `grp`. The reference program is written for one: setup_inputs(seed, part) draws one part's arguments, and reference() takes and returns one part's arrays. A program takes and returns all parts, laid end to end along the dimension named above; an argument that names none is the same for every part. Nothing has to cross between parts.
Inputs may be any that keep to these rules, and one draw needn't show every extreme that they name: Each value appears once; device d holds the segments pair_of[d] and 127 - pair_of[d], each of 256 tokens.
All inputs are finite; a program needn't handle non-finite values.
Results may differ from the reference program's by a relative error of at most 0.0058.
Values may be sent and summed in bfloat16 or wider, within the bound.
A program may use at most 128 MiB of HBM per device.

```python
import jax
import jax.numpy as jnp
from jax import lax

H = 8
HD = 128
SEGMENT = 256
STEPS = 4
TOKENS = 32768
N_CTX = 64


def level_of(key, dims, cuts, least, top_value):
    loudness = 1.0
    for axis_at, shards_of in cuts:
        steps = jax.random.uniform(jax.random.fold_in(jax.random.fold_in(key, 6), axis_at), (shards_of,), jnp.float32, least / len(cuts), top_value / len(cuts))
        loudness = loudness * jnp.repeat(jnp.exp(steps), dims[axis_at] // shards_of).reshape((-1,) + (1,) * (len(dims) - 1 - axis_at))
    return loudness


def scatter_about(stream_key, dims, scale, bound, shards=(), held_as=jnp.bfloat16):
    array = scale * jax.random.normal(stream_key, dims, jnp.float32)
    if shards:
        array = array * level_of(stream_key, dims, shards, -0.22, 0.18)
    return jnp.clip(array, -bound, bound).astype(held_as)


def setup_inputs(seed: int = 0, part: int = 0) -> dict:
    splits = jax.random.split(jax.random.key(seed), 8)
    part_splits = jax.random.split(jax.random.fold_in(splits[7], part), 8)
    return {
        "queries": scatter_about(part_splits[0], (TOKENS, H * HD), 1.0, 6.0, ((0, 64),)),
        "keys": scatter_about(part_splits[1], (TOKENS, HD), 1.0, 6.0, ((0, 64),)),
        "values": scatter_about(part_splits[2], (TOKENS, HD), 1.0, 6.0, ((0, 64),)),
        "outputs": scatter_about(part_splits[3], (TOKENS, H * HD), 1.0, 6.0, ((0, 64),)),
        "out_grad": scatter_about(part_splits[4], (TOKENS, H * HD), 1.0, 6.0, ((0, 64),)),
        "log_sums": jnp.clip(3.0 + 3.0 * jax.random.uniform(part_splits[5], (H, TOKENS), jnp.float32) ** level_of(part_splits[5], (H, TOKENS), ((1, 64),), -0.2, 0.2), 3.0, 6.0),
        "pair_of": jax.random.permutation(splits[6], N_CTX).astype(jnp.int32),
    }


def tile_grads(q_rows, g_rows, lse_rows, delta_rows, q_pos, key_rows, value_rows, k_pos):
    row_count = q_rows.shape[0]
    head_count = lse_rows.shape[0]
    head_dim = key_rows.shape[1]
    factor = head_dim ** -0.5
    q_heads = q_rows.reshape(row_count, head_count, head_dim).astype(jnp.float32)
    g_heads = g_rows.reshape(row_count, head_count, head_dim).astype(jnp.float32)
    key_full = key_rows.astype(jnp.float32)
    value_full = value_rows.astype(jnp.float32)
    scores = jnp.einsum("qhd,kd->hqk", q_heads, key_full) * factor
    allowed = k_pos[None, None, :] <= q_pos[None, :, None]
    probs = jnp.where(allowed, jnp.exp(scores - lse_rows[:, :, None]), 0.0)
    dprobs = jnp.einsum("qhd,kd->hqk", g_heads, value_full)
    dscores = lax.optimization_barrier((probs * (dprobs - delta_rows[:, :, None])).astype(jnp.bfloat16)).astype(jnp.float32)
    probs_low = lax.optimization_barrier(probs.astype(jnp.bfloat16)).astype(jnp.float32)
    grad_v = jnp.einsum("hqk,qhd->kd", probs_low, g_heads)
    grad_k = jnp.einsum("hqk,qhd->kd", dscores, q_heads) * factor
    grad_q = jnp.einsum("hqk,kd->qhd", dscores, key_full) * factor
    return grad_q.reshape(row_count, head_count * head_dim), grad_k, grad_v


def pair_grads(q_rows, g_rows, lse_rows, delta_rows, q_segs, key_rows, value_rows, k_segs, seg_len):
    offsets = jnp.arange(seg_len, dtype=jnp.int32)
    width_q = q_rows.shape[1]
    head_dim = key_rows.shape[1]
    pieces_q = []
    sums_k = [jnp.zeros((seg_len, head_dim), jnp.float32), jnp.zeros((seg_len, head_dim), jnp.float32)]
    sums_v = [jnp.zeros((seg_len, head_dim), jnp.float32), jnp.zeros((seg_len, head_dim), jnp.float32)]
    for q_half in range(2):
        q_part = slice(q_half * seg_len, (q_half + 1) * seg_len)
        total_q = jnp.zeros((seg_len, width_q), jnp.float32)
        for k_half in range(2):
            k_part = slice(k_half * seg_len, (k_half + 1) * seg_len)

            def live_tile():
                return tile_grads(q_rows[q_part], g_rows[q_part], lse_rows[:, q_part], delta_rows[:, q_part],
                                  q_segs[q_half] * seg_len + offsets, key_rows[k_part], value_rows[k_part],
                                  k_segs[k_half] * seg_len + offsets)

            def dead_tile():
                return (jnp.zeros((seg_len, width_q), jnp.float32), jnp.zeros((seg_len, head_dim), jnp.float32),
                        jnp.zeros((seg_len, head_dim), jnp.float32))

            part_q, part_k, part_v = lax.cond(k_segs[k_half] <= q_segs[q_half], live_tile, dead_tile)
            total_q = total_q + part_q
            sums_k[k_half] = sums_k[k_half] + part_k
            sums_v[k_half] = sums_v[k_half] + part_v
        pieces_q.append(total_q)
    return (jnp.concatenate(pieces_q, axis=0), jnp.concatenate(sums_k, axis=0), jnp.concatenate(sums_v, axis=0))


def reference(queries, keys, values, outputs, out_grad, log_sums, pair_of):
    block = 2 * SEGMENT
    head_dim = keys.shape[1]
    head_count = log_sums.shape[0]
    delta_all = jnp.sum((out_grad.astype(jnp.float32) * outputs.astype(jnp.float32)).reshape(TOKENS, head_count, head_dim), axis=2).T

    def segments_of(holder):
        first = pair_of[holder]
        return jnp.stack([first, 2 * N_CTX - 1 - first]).astype(jnp.int32)

    def visit(carry, device):
        acc_k, acc_v = carry
        start = (device * block).astype(jnp.int32)
        q_rows = lax.dynamic_slice_in_dim(queries, start, block, 0)
        g_rows = lax.dynamic_slice_in_dim(out_grad, start, block, 0)
        lse_rows = lax.dynamic_slice_in_dim(log_sums, start, block, 1)
        delta_rows = lax.dynamic_slice_in_dim(delta_all, start, block, 1)
        own_segs = segments_of(device)
        total_q = jnp.zeros((block, queries.shape[1]), jnp.float32)
        for hop_index in range(STEPS):
            source = ((device - hop_index) % N_CTX).astype(jnp.int32)
            k_start = (source * block).astype(jnp.int32)
            key_rows = lax.dynamic_slice_in_dim(keys, k_start, block, 0)
            value_rows = lax.dynamic_slice_in_dim(values, k_start, block, 0)
            part_q, part_k, part_v = pair_grads(q_rows, g_rows, lse_rows, delta_rows, own_segs,
                                                key_rows, value_rows, segments_of(source), SEGMENT)
            total_q = total_q + part_q
            acc_k = lax.dynamic_update_slice_in_dim(acc_k, lax.dynamic_slice_in_dim(acc_k, k_start, block, 0) + part_k, k_start, 0)
            acc_v = lax.dynamic_update_slice_in_dim(acc_v, lax.dynamic_slice_in_dim(acc_v, k_start, block, 0) + part_v, k_start, 0)
        return (acc_k, acc_v), total_q.astype(jnp.bfloat16)

    start_state = (jnp.zeros((TOKENS, head_dim), jnp.float32), jnp.zeros((TOKENS, head_dim), jnp.float32))
    finals, blocks_q = lax.scan(visit, start_state, jnp.arange(N_CTX, dtype=jnp.int32))
    return blocks_q.reshape(TOKENS, queries.shape[1]), finals[0], finals[1]
```

```python
import jax
import jax.numpy as jnp
from jax import lax
from jax.experimental import pallas as pl
from jax.experimental.pallas import tpu as pltpu
from jax.sharding import PartitionSpec as P

MESH = pl.DeviceIdType.MESH
LOG2E = 1.4426950408889634
SEG = 256
HEADS = 8
DIM = 128
ROWS = HEADS * SEG
FACTOR = DIM**-0.5


def dot_nt(a, b):
    return lax.dot_general(a, b, (((1,), (1,)), ((), ())), preferred_element_type=jnp.float32)


def dot_nn(a, b):
    return lax.dot_general(a, b, (((1,), (0,)), ((), ())), preferred_element_type=jnp.float32)


def kernel(
    ctx_count,
    pair_ref, q_hbm, k_ref, v_ref, o_hbm, g_hbm, lse_ref,
    dq_hbm, dk_ref, dv_ref,
    q_in, g_in, o_in,
    q_t, g_t, lse_b, delta_b,
    k1, k2, k3, v1, v2, v3,
    probs, dsc,
    dq_acc, dq_out, own_v, own_k, sent_v, sent_k, got_v, got_k,
    in_sem, out_sem,
    k_send, k_recv, v_send, v_recv, gv_send, gv_recv, gk_send, gk_recv,
):
    me = lax.axis_index("ctx")
    right = lax.rem(me + 1, ctx_count)
    left = lax.rem(me + ctx_count - 1, ctx_count)

    barrier = pltpu.get_barrier_semaphore()
    for peer in (left, right):
        pl.semaphore_signal(barrier, inc=1, device_id={"ctx": peer}, device_id_type=MESH)

    loads = []
    for i, (src, dst) in enumerate(((q_hbm, q_in), (g_hbm, g_in), (o_hbm, o_in))):
        for sg in range(2):
            load = pltpu.make_async_copy(src.at[pl.ds(sg * SEG, SEG)], dst.at[sg], in_sem.at[i, sg])
            load.start()
            loads.append(load)

    keys = [None, k1, k2, k3]
    values = [None, v1, v2, v3]

    def forward(bufs, first, step, seg, send, recv):
        src = first.at[pl.ds(seg * SEG, SEG)] if step == 0 else bufs[step].at[seg]
        return pltpu.make_async_remote_copy(
            src_ref=src,
            dst_ref=bufs[step + 1].at[seg],
            send_sem=send.at[step, seg],
            recv_sem=recv.at[step, seg],
            device_id={"ctx": right},
            device_id_type=MESH,
        )

    key_copy = [[forward(keys, k_ref, s, g, k_send, k_recv) for g in range(2)] for s in range(3)]
    value_copy = [[forward(values, v_ref, s, g, v_send, v_recv) for g in range(2)] for s in range(3)]

    def back(sent, got, step, seg, send, recv):
        return pltpu.make_async_remote_copy(
            src_ref=sent.at[step - 1, seg],
            dst_ref=got.at[step - 1, seg],
            send_sem=send.at[step - 1, seg],
            recv_sem=recv.at[step - 1, seg],
            device_id={"ctx": left},
            device_id_type=MESH,
        )

    gv_copy = [None] + [[back(sent_v, got_v, s, g, gv_send, gv_recv) for g in range(2)] for s in (1, 2, 3)]
    gk_copy = [None] + [[back(sent_k, got_k, s, g, gk_send, gk_recv) for g in range(2)] for s in (1, 2, 3)]

    pl.semaphore_wait(barrier, 2)
    key_copy[0][0].start()
    key_copy[0][1].start()
    value_copy[0][0].start()

    for load in loads:
        load.wait()
    for h in range(HEADS):
        cols = slice(h * DIM, (h + 1) * DIM)
        for sg in range(2):
            qh = q_in[sg, :, cols]
            gh = g_in[sg, :, cols]
            q_t[sg, :, h * SEG : (h + 1) * SEG] = qh.T
            g_t[sg, :, h * SEG : (h + 1) * SEG] = gh.T
            delta = jnp.sum(
                gh.astype(jnp.float32) * o_in[sg, :, cols].astype(jnp.float32), axis=1, keepdims=True
            )
            delta_b[sg, h * SEG : (h + 1) * SEG, :] = jnp.broadcast_to(delta, (SEG, DIM))
            for j in range(SEG // DIM):
                at = sg * SEG + j * DIM
                row = lse_ref[h : h + 1, at : at + DIM] * LOG2E
                lse_b[sg, h * SEG + j * DIM : h * SEG + (j + 1) * DIM, :] = jnp.broadcast_to(row, (DIM, DIM)).T

    def wide(x):
        return jnp.concatenate([x, x], axis=1)

    def probs_of(q_seg, key, out, diagonal):
        for h in range(HEADS):
            rows = pl.ds(h * SEG, SEG)
            qh = q_heads(q_seg, h)
            x = dot_nt(qh, key) * (FACTOR * LOG2E) - wide(lse_b[q_seg, rows, :])
            p = jnp.exp2(x)
            if diagonal:
                below = lax.broadcasted_iota(jnp.int32, (SEG, SEG), 1) <= lax.broadcasted_iota(
                    jnp.int32, (SEG, SEG), 0
                )
                p = jnp.where(below, p, 0.0)
            out[rows, :] = p.astype(jnp.bfloat16)

    def dscores_of(q_seg, value, pin, out):
        for h in range(HEADS):
            rows = pl.ds(h * SEG, SEG)
            dp = dot_nt(g_heads(q_seg, h), value)
            ds = pin[rows, :].astype(jnp.float32) * (dp - wide(delta_b[q_seg, rows, :]))
            out[rows, :] = ds.astype(jnp.bfloat16)

    def q_heads(q_seg, h):
        return q_in[q_seg, :, h * DIM : (h + 1) * DIM]

    def g_heads(q_seg, h):
        return g_in[q_seg, :, h * DIM : (h + 1) * DIM]

    def own_tile(q_seg, k_seg, diagonal, first_q, first_k):
        key = k_ref[k_seg * SEG : (k_seg + 1) * SEG, :]
        value = v_ref[k_seg * SEG : (k_seg + 1) * SEG, :]
        p, d = probs.at[0, 0], dsc.at[0]
        probs_of(q_seg, key, p, diagonal)
        dscores_of(q_seg, value, p, d)
        part_v = dot_nn(g_t[q_seg], p[...])
        part_k = dot_nn(q_t[q_seg], d[...])
        part_q = dot_nn(d[...], key)
        if first_k:
            own_v[0, k_seg] = part_v
            own_k[0, k_seg] = part_k
        else:
            own_v[0, k_seg] += part_v
            own_k[0, k_seg] += part_k
        if first_q:
            dq_acc[q_seg] = part_q
        else:
            dq_acc[q_seg] += part_q

    mine = pair_ref[me]
    b_seg = [None] + [
        lax.div(pair_ref[lax.rem(me + ctx_count - s, ctx_count)] - mine + ctx_count, ctx_count) for s in (1, 2, 3)
    ]

    def pick(step, earlier, later):
        return jnp.where(jnp.broadcast_to(b_seg[step], earlier.shape) == 0, earlier, later)

    def spread(own, step, part_a, part_b):
        zero = jnp.zeros_like(part_b)
        own[step, 0] = part_a + pick(step, part_b, zero)
        own[step, 1] = pick(step, zero, part_b)

    def stage_v(s):
        qb = b_seg[s]
        key_a = keys[s][0]
        key_b = pick(s, key_a, keys[s][1])
        probs_of(1, key_a, probs.at[s, 0], False)
        probs_of(qb, key_b, probs.at[s, 1], False)
        spread(own_v, s, dot_nn(g_t[1], probs[s, 0]), dot_nn(g_t[qb], probs[s, 1]))

    def stage_k(s):
        qb = b_seg[s]
        key_a = keys[s][0]
        key_b = pick(s, key_a, keys[s][1])
        value_a = values[s][0]
        value_b = pick(s, value_a, values[s][1])
        dscores_of(1, value_a, probs.at[s, 0], dsc.at[0])
        dscores_of(qb, value_b, probs.at[s, 1], dsc.at[1])
        spread(own_k, s, dot_nn(q_t[1], dsc[0]), dot_nn(q_t[qb], dsc[1]))

        def rest():
            part_b = dot_nn(dsc[1], key_b)
            zero = jnp.zeros_like(part_b)
            dq_acc[1] += dot_nn(dsc[0], key_a) + pick(s, zero, part_b)
            dq_acc[0] += pick(s, part_b, zero)

        return rest

    def pass_back(copies, own, sent, got, s, seg):
        total = own[s, seg]
        if s < 3:
            copies[s + 1][seg].wait_recv()
            total = total + got[s, seg].astype(jnp.float32)
        sent[s - 1, seg] = total.astype(jnp.bfloat16)
        copies[s][seg].start()

    def finish(copies, own, got, seg, scale, out):
        copies[1][seg].wait_recv()
        total = own[0, seg] + got[0, seg].astype(jnp.float32)
        if scale is not None:
            total = total * scale
        out[seg * SEG : (seg + 1) * SEG, :] = total.T

    def arrived(copies, step, seg):
        copies[step - 1][seg].wait_recv()
        if step < 3:
            copies[step][seg].start()

    arrived(key_copy, 1, 0)
    arrived(key_copy, 1, 1)
    value_copy[0][1].start()
    own_tile(1, 0, False, True, True)
    own_tile(0, 0, True, True, False)
    arrived(key_copy, 2, 0)
    arrived(key_copy, 2, 1)
    arrived(value_copy, 1, 0)
    stage_v(1)
    arrived(value_copy, 1, 1)
    stage_v(2)
    own_tile(1, 1, True, False, True)
    arrived(key_copy, 3, 0)
    arrived(key_copy, 3, 1)
    stage_v(3)
    for seg in range(2):
        pass_back(gv_copy, own_v, sent_v, got_v, 3, seg)
    arrived(value_copy, 2, 0)
    arrived(value_copy, 2, 1)
    stage_k(1)()
    for seg in range(2):
        pass_back(gv_copy, own_v, sent_v, got_v, 2, seg)
    stage_k(2)()
    arrived(value_copy, 3, 0)
    arrived(value_copy, 3, 1)
    rest = stage_k(3)
    for seg in range(2):
        pass_back(gk_copy, own_k, sent_k, got_k, 3, seg)
    for seg in range(2):
        pass_back(gv_copy, own_v, sent_v, got_v, 1, seg)
    rest()
    for h in range(HEADS):
        for sg in range(2):
            dq_out[sg * SEG : (sg + 1) * SEG, h * DIM : (h + 1) * DIM] = (
                dq_acc[sg, h * SEG : (h + 1) * SEG, :] * FACTOR
            ).astype(jnp.bfloat16)
    store = pltpu.make_async_copy(dq_out, dq_hbm, out_sem)
    store.start()
    for seg in range(2):
        pass_back(gk_copy, own_k, sent_k, got_k, 2, seg)
    for seg in range(2):
        finish(gv_copy, own_v, got_v, seg, None, dv_ref)
    for seg in range(2):
        pass_back(gk_copy, own_k, sent_k, got_k, 1, seg)
    for seg in range(2):
        finish(gk_copy, own_k, got_k, seg, FACTOR, dk_ref)
    store.wait()
    for copies in (key_copy, value_copy, gv_copy[1:], gk_copy[1:]):
        for pair in copies:
            for copy in pair:
                copy.wait_send()


def per_device(queries, keys, values, outputs, out_grad, log_sums, pair_of):
    ctx_count = lax.axis_size("ctx")
    bf16, f32 = jnp.bfloat16, jnp.float32
    vmem = pl.BlockSpec(memory_space=pltpu.VMEM)
    hbm = pl.BlockSpec(memory_space=pl.ANY)
    smem = pl.BlockSpec(memory_space=pltpu.SMEM)
    sems = pltpu.SemaphoreType.DMA((3, 2))

    def body(*refs):
        kernel(ctx_count, *refs)

    return pl.pallas_call(
        body,
        out_shape=(
            jax.ShapeDtypeStruct(queries.shape, bf16),
            jax.ShapeDtypeStruct(keys.shape, f32),
            jax.ShapeDtypeStruct(values.shape, f32),
        ),
        in_specs=[smem, hbm, vmem, vmem, hbm, hbm, vmem],
        out_specs=(hbm, vmem, vmem),
        scratch_shapes=[
            pltpu.VMEM((2, SEG, HEADS * DIM), bf16),
            pltpu.VMEM((2, SEG, HEADS * DIM), bf16),
            pltpu.VMEM((2, SEG, HEADS * DIM), bf16),
            pltpu.VMEM((2, DIM, ROWS), bf16),
            pltpu.VMEM((2, DIM, ROWS), bf16),
            pltpu.VMEM((2, ROWS, DIM), f32),
            pltpu.VMEM((2, ROWS, DIM), f32),
        ]
        + [pltpu.VMEM((2, SEG, DIM), bf16)] * 6
        + [
            pltpu.VMEM((4, 2, ROWS, SEG), bf16),
            pltpu.VMEM((2, ROWS, SEG), bf16),
            pltpu.VMEM((2, ROWS, DIM), f32),
            pltpu.VMEM((2 * SEG, HEADS * DIM), bf16),
            pltpu.VMEM((4, 2, DIM, SEG), f32),
            pltpu.VMEM((4, 2, DIM, SEG), f32),
            pltpu.VMEM((3, 2, DIM, SEG), bf16),
            pltpu.VMEM((3, 2, DIM, SEG), bf16),
            pltpu.VMEM((3, 2, DIM, SEG), bf16),
            pltpu.VMEM((3, 2, DIM, SEG), bf16),
            pltpu.SemaphoreType.DMA((3, 2)),
            pltpu.SemaphoreType.DMA,
        ]
        + [sems] * 8,
        compiler_params=pltpu.CompilerParams(
            collective_id=0, has_side_effects=True, vmem_limit_bytes=56 * 2**20
        ),
        cost_estimate=pl.CostEstimate(
            flops=6_000_000_000, bytes_accessed=5_000_000, transcendentals=4_700_000
        ),
        name="gqa_backward",
    )(pair_of, queries, keys, values, outputs, out_grad, log_sums)


def solution(mesh):
    return jax.shard_map(
        per_device,
        mesh=mesh,
        in_specs=(
            P("ctx", "grp"),
            P("ctx", "grp"),
            P("ctx", "grp"),
            P("ctx", "grp"),
            P("ctx", "grp"),
            P("grp", "ctx"),
            P(),
        ),
        out_specs=(P("ctx", "grp"), P("ctx", "grp"), P("ctx", "grp")),
        check_vma=False,
    )
```

```python
import jax
import jax.numpy as jnp
from jax import lax
from jax.experimental import pallas as pl
from jax.experimental.pallas import tpu as pltpu
from jax.sharding import PartitionSpec as P

MESH = pl.DeviceIdType.MESH
LOG2E = 1.4426950408889634
SEG = 256
HEADS = 8
DIM = 128
ROWS = HEADS * SEG
FACTOR = DIM**-0.5


def dot_nt(a, b):
    return lax.dot_general(a, b, (((1,), (1,)), ((), ())), preferred_element_type=jnp.float32)


def dot_nn(a, b):
    return lax.dot_general(a, b, (((1,), (0,)), ((), ())), preferred_element_type=jnp.float32)


def kernel(
    ctx_count,
    pair_hbm, q_hbm, k_hbm, v_hbm, o_hbm, g_hbm, lse_hbm,
    dq_ref, dk_ref, dv_ref,
    pair_ref, k_ref, v_ref, lse_ref, q_in, g_in, o_in,
    q_t, g_t, lse_b, delta_b,
    k1, k2, k3, v1, v2, v3,
    probs, dsc,
    dq_acc, own_v, own_k, sent_v, sent_k, got_v, got_k,
    in_sem, small_sem,
    k_send, k_recv, v_send, v_recv, gv_send, gv_recv, gk_send, gk_recv,
):
    me = lax.axis_index("ctx")
    right = lax.rem(me + 1, ctx_count)
    left = lax.rem(me + ctx_count - 1, ctx_count)

    barrier = pltpu.get_barrier_semaphore()
    for peer in (left, right):
        pl.semaphore_signal(barrier, inc=1, device_id={"ctx": peer}, device_id_type=MESH)

    loads = []
    for i, (src, dst) in enumerate(((q_hbm, q_in), (g_hbm, g_in), (o_hbm, o_in))):
        for sg in range(2):
            load = pltpu.make_async_copy(src.at[pl.ds(sg * SEG, SEG)], dst.at[sg], in_sem.at[i, sg])
            load.start()
            loads.append(load)
    for i, (src, dst) in enumerate(((pair_hbm, pair_ref), (k_hbm, k_ref), (v_hbm, v_ref), (lse_hbm, lse_ref))):
        load = pltpu.make_async_copy(src, dst, small_sem.at[i])
        load.start()
        loads.append(load)

    keys = [None, k1, k2, k3]
    values = [None, v1, v2, v3]

    def forward(bufs, first, step, seg, send, recv):
        src = first.at[pl.ds(seg * SEG, SEG)] if step == 0 else bufs[step].at[seg]
        return pltpu.make_async_remote_copy(
            src_ref=src,
            dst_ref=bufs[step + 1].at[seg],
            send_sem=send.at[step, seg],
            recv_sem=recv.at[step, seg],
            device_id={"ctx": right},
            device_id_type=MESH,
        )

    key_copy = [[forward(keys, k_hbm, s, g, k_send, k_recv) for g in range(2)] for s in range(3)]
    value_copy = [[forward(values, v_hbm, s, g, v_send, v_recv) for g in range(2)] for s in range(3)]

    def back(sent, got, step, seg, send, recv):
        return pltpu.make_async_remote_copy(
            src_ref=sent.at[step - 1, seg],
            dst_ref=got.at[step - 1, seg],
            send_sem=send.at[step - 1, seg],
            recv_sem=recv.at[step - 1, seg],
            device_id={"ctx": left},
            device_id_type=MESH,
        )

    gv_copy = [None] + [[back(sent_v, got_v, s, g, gv_send, gv_recv) for g in range(2)] for s in (1, 2, 3)]
    gk_copy = [None] + [[back(sent_k, got_k, s, g, gk_send, gk_recv) for g in range(2)] for s in (1, 2, 3)]

    pl.semaphore_wait(barrier, 2)

    def prologue():
        for load in loads:
            load.wait()
        for h in range(HEADS):
            cols = slice(h * DIM, (h + 1) * DIM)
            for sg in range(2):
                qh = q_in[sg, :, cols]
                gh = g_in[sg, :, cols]
                q_t[sg, :, h * SEG : (h + 1) * SEG] = qh.T
                g_t[sg, :, h * SEG : (h + 1) * SEG] = gh.T
                delta = jnp.sum(
                    gh.astype(jnp.float32) * o_in[sg, :, cols].astype(jnp.float32), axis=1, keepdims=True
                )
                delta_b[sg, h * SEG : (h + 1) * SEG, :] = jnp.broadcast_to(delta, (SEG, DIM))
                for j in range(SEG // DIM):
                    at = sg * SEG + j * DIM
                    row = lse_ref[h : h + 1, at : at + DIM] * LOG2E
                    lse_b[sg, h * SEG + j * DIM : h * SEG + (j + 1) * DIM, :] = jnp.broadcast_to(row, (DIM, DIM)).T
        dq_acc[...] = jnp.zeros_like(dq_acc)

    def wide(x):
        return jnp.concatenate([x, x], axis=1)

    def probs_of(q_seg, key, out, diagonal):
        for h in range(HEADS):
            rows = pl.ds(h * SEG, SEG)
            qh = q_heads(q_seg, h)
            x = dot_nt(qh, key) * (FACTOR * LOG2E) - wide(lse_b[q_seg, rows, :])
            p = jnp.exp2(x)
            if diagonal:
                below = lax.broadcasted_iota(jnp.int32, (SEG, SEG), 1) <= lax.broadcasted_iota(
                    jnp.int32, (SEG, SEG), 0
                )
                p = jnp.where(below, p, 0.0)
            out[rows, :] = p.astype(jnp.bfloat16)

    def dscores_of(q_seg, value, pin, out):
        for h in range(HEADS):
            rows = pl.ds(h * SEG, SEG)
            dp = dot_nt(g_heads(q_seg, h), value)
            ds = pin[rows, :].astype(jnp.float32) * (dp - wide(delta_b[q_seg, rows, :]))
            out[rows, :] = ds.astype(jnp.bfloat16)

    def q_heads(q_seg, h):
        return q_in[q_seg, :, h * DIM : (h + 1) * DIM]

    def g_heads(q_seg, h):
        return g_in[q_seg, :, h * DIM : (h + 1) * DIM]

    def own_probs(q_seg, k_seg, diagonal):
        probs_of(q_seg, k_ref[k_seg * SEG : (k_seg + 1) * SEG, :], probs.at[0, 0], diagonal)

    def own_rest(q_seg, k_seg, first_k):
        key = k_ref[k_seg * SEG : (k_seg + 1) * SEG, :]
        value = v_ref[k_seg * SEG : (k_seg + 1) * SEG, :]
        p, d = probs.at[0, 0], dsc.at[0]
        dscores_of(q_seg, value, p, d)
        part_v = dot_nn(g_t[q_seg], p[...])
        part_k = dot_nn(q_t[q_seg], d[...])
        part_q = dot_nn(d[...], key)
        if first_k:
            own_v[0, k_seg] = part_v
            own_k[0, k_seg] = part_k
        else:
            own_v[0, k_seg] += part_v
            own_k[0, k_seg] += part_k
        dq_acc[q_seg] += part_q

    def pick(step, earlier, later):
        return jnp.where(jnp.broadcast_to(b_seg[step], earlier.shape) == 0, earlier, later)

    def spread(own, step, part_a, part_b):
        zero = jnp.zeros_like(part_b)
        own[step, 0] = part_a + pick(step, part_b, zero)
        own[step, 1] = pick(step, zero, part_b)

    def stage_v(s):
        qb = b_seg[s]
        key_a = keys[s][0]
        key_b = pick(s, key_a, keys[s][1])
        probs_of(1, key_a, probs.at[s, 0], False)
        probs_of(qb, key_b, probs.at[s, 1], False)
        spread(own_v, s, dot_nn(g_t[1], probs[s, 0]), dot_nn(g_t[qb], probs[s, 1]))

    def stage_k(s):
        qb = b_seg[s]
        value_a = values[s][0]
        value_b = pick(s, value_a, values[s][1])
        dscores_of(1, value_a, probs.at[s, 0], dsc.at[0])
        dscores_of(qb, value_b, probs.at[s, 1], dsc.at[1])
        spread(own_k, s, dot_nn(q_t[1], dsc[0]), dot_nn(q_t[qb], dsc[1]))

    def queries_of(s):
        key_a = keys[s][0]
        part_b = dot_nn(dsc[1], pick(s, key_a, keys[s][1]))
        zero = jnp.zeros_like(part_b)
        dq_acc[1] += dot_nn(dsc[0], key_a) + pick(s, zero, part_b)
        dq_acc[0] += pick(s, part_b, zero)

    def scaled_queries():
        for h in range(HEADS):
            for sg in range(2):
                dq_ref[sg * SEG : (sg + 1) * SEG, h * DIM : (h + 1) * DIM] = (
                    dq_acc[sg, h * SEG : (h + 1) * SEG, :] * FACTOR
                ).astype(jnp.bfloat16)

    def pass_back(copies, own, sent, got, s, seg):
        total = own[s, seg]
        if s < 3:
            copies[s + 1][seg].wait_recv()
            total = total + got[s, seg].astype(jnp.float32)
        sent[s - 1, seg] = total.astype(jnp.bfloat16)
        copies[s][seg].start()

    def finish(copies, own, got, seg, scale, out):
        copies[1][seg].wait_recv()
        total = own[0, seg] + got[0, seg].astype(jnp.float32)
        if scale is not None:
            total = total * scale
        out[seg * SEG : (seg + 1) * SEG, :] = total.T

    def arrived(copies, step, seg):
        copies[step - 1][seg].wait_recv()
        if step < 3:
            copies[step][seg].start()

    key_copy[0][0].start()
    key_copy[0][1].start()
    value_copy[0][0].start()
    prologue()
    mine = pair_ref[me]
    b_seg = [None] + [
        lax.div(pair_ref[lax.rem(me + ctx_count - s, ctx_count)] - mine + ctx_count, ctx_count) for s in (1, 2, 3)
    ]
    arrived(key_copy, 1, 0)
    arrived(key_copy, 1, 1)
    own_probs(1, 0, False)
    value_copy[0][1].start()
    arrived(key_copy, 2, 0)
    arrived(key_copy, 2, 1)
    arrived(value_copy, 1, 0)
    arrived(value_copy, 1, 1)
    stage_v(2)
    arrived(key_copy, 3, 0)
    stage_v(1)
    arrived(key_copy, 3, 1)
    stage_v(3)
    arrived(value_copy, 2, 0)
    pass_back(gv_copy, own_v, sent_v, got_v, 3, 0)
    own_rest(1, 0, True)
    pass_back(gv_copy, own_v, sent_v, got_v, 3, 1)
    arrived(value_copy, 2, 1)
    stage_k(1)
    pass_back(gv_copy, own_v, sent_v, got_v, 2, 0)
    arrived(value_copy, 3, 0)
    queries_of(1)
    own_probs(0, 0, True)
    pass_back(gv_copy, own_v, sent_v, got_v, 2, 1)
    arrived(value_copy, 3, 1)
    stage_k(3)
    pass_back(gk_copy, own_k, sent_k, got_k, 3, 0)
    pass_back(gk_copy, own_k, sent_k, got_k, 3, 1)
    queries_of(3)
    pass_back(gv_copy, own_v, sent_v, got_v, 1, 0)
    own_rest(0, 0, False)
    stage_k(2)
    pass_back(gk_copy, own_k, sent_k, got_k, 2, 0)
    queries_of(2)
    pass_back(gk_copy, own_k, sent_k, got_k, 2, 1)
    pass_back(gv_copy, own_v, sent_v, got_v, 1, 1)
    own_probs(1, 1, True)
    pass_back(gk_copy, own_k, sent_k, got_k, 1, 0)
    finish(gv_copy, own_v, got_v, 0, None, dv_ref)
    pass_back(gk_copy, own_k, sent_k, got_k, 1, 1)
    own_rest(1, 1, True)
    finish(gv_copy, own_v, got_v, 1, None, dv_ref)
    finish(gk_copy, own_k, got_k, 0, FACTOR, dk_ref)
    scaled_queries()
    finish(gk_copy, own_k, got_k, 1, FACTOR, dk_ref)
    for copies in (key_copy, value_copy, gv_copy[1:], gk_copy[1:]):
        for pair in copies:
            for copy in pair:
                copy.wait_send()


def per_device(queries, keys, values, outputs, out_grad, log_sums, pair_of):
    ctx_count = lax.axis_size("ctx")
    bf16, f32 = jnp.bfloat16, jnp.float32
    vmem = pl.BlockSpec(memory_space=pltpu.VMEM)
    hbm = pl.BlockSpec(memory_space=pltpu.HBM)
    sems = pltpu.SemaphoreType.DMA((3, 2))

    def body(*refs):
        kernel(ctx_count, *refs)

    grads = pl.pallas_call(
        body,
        out_shape=(
            jax.ShapeDtypeStruct(queries.shape, bf16),
            jax.ShapeDtypeStruct(keys.shape, f32),
            jax.ShapeDtypeStruct(values.shape, f32),
        ),
        in_specs=[hbm] * 7,
        out_specs=(vmem, vmem, vmem),
        scratch_shapes=[
            pltpu.SMEM(pair_of.shape, jnp.int32),
            pltpu.VMEM(keys.shape, bf16),
            pltpu.VMEM(values.shape, bf16),
            pltpu.VMEM(log_sums.shape, f32),
            pltpu.VMEM((2, SEG, HEADS * DIM), bf16),
            pltpu.VMEM((2, SEG, HEADS * DIM), bf16),
            pltpu.VMEM((2, SEG, HEADS * DIM), bf16),
            pltpu.VMEM((2, DIM, ROWS), bf16),
            pltpu.VMEM((2, DIM, ROWS), bf16),
            pltpu.VMEM((2, ROWS, DIM), f32),
            pltpu.VMEM((2, ROWS, DIM), f32),
        ]
        + [pltpu.VMEM((2, SEG, DIM), bf16)] * 6
        + [
            pltpu.VMEM((4, 2, ROWS, SEG), bf16),
            pltpu.VMEM((2, ROWS, SEG), bf16),
            pltpu.VMEM((2, ROWS, DIM), f32),
            pltpu.VMEM((4, 2, DIM, SEG), f32),
            pltpu.VMEM((4, 2, DIM, SEG), f32),
            pltpu.VMEM((3, 2, DIM, SEG), bf16),
            pltpu.VMEM((3, 2, DIM, SEG), bf16),
            pltpu.VMEM((3, 2, DIM, SEG), bf16),
            pltpu.VMEM((3, 2, DIM, SEG), bf16),
            pltpu.SemaphoreType.DMA((3, 2)),
            pltpu.SemaphoreType.DMA((4,)),
        ]
        + [sems] * 8,
        compiler_params=pltpu.CompilerParams(
            collective_id=0, has_side_effects=True, vmem_limit_bytes=40 * 2**20
        ),
        cost_estimate=pl.CostEstimate(
            flops=6_000_000_000, bytes_accessed=5_000_000, transcendentals=4_700_000
        ),
        name="gqa_backward",
    )(*(pltpu.with_memory_space_constraint(x, pltpu.HBM) for x in (pair_of, queries, keys, values, outputs, out_grad, log_sums)))

    def written(dq_ref, dk_ref, dv_ref, dq_hbm, dk_hbm, dv_hbm, sem):
        copies = [
            pltpu.make_async_copy(src, dst, sem.at[i])
            for i, (src, dst) in enumerate(((dq_ref, dq_hbm), (dk_ref, dk_hbm), (dv_ref, dv_hbm)))
        ]
        for copy in copies:
            copy.start()
        for copy in copies:
            copy.wait()

    return pl.pallas_call(
        written,
        out_shape=tuple(jax.ShapeDtypeStruct(x.shape, x.dtype) for x in grads),
        in_specs=[vmem] * 3,
        out_specs=(hbm,) * 3,
        scratch_shapes=[pltpu.SemaphoreType.DMA((3,))],
        compiler_params=pltpu.CompilerParams(vmem_limit_bytes=8 * 2**20),
        name="written",
    )(*grads)


def solution(mesh):
    return jax.shard_map(
        per_device,
        mesh=mesh,
        in_specs=(
            P("ctx", "grp"),
            P("ctx", "grp"),
            P("ctx", "grp"),
            P("ctx", "grp"),
            P("ctx", "grp"),
            P("grp", "ctx"),
            P(),
        ),
        out_specs=(P("ctx", "grp"), P("ctx", "grp"), P("ctx", "grp")),
        check_vma=False,
    )
```

```python
import jax
import jax.numpy as jnp
from jax import lax
from jax.experimental import pallas as pl
from jax.experimental.pallas import tpu as pltpu
from jax.sharding import PartitionSpec as P

MESH = pl.DeviceIdType.MESH
LOG2E = 1.4426950408889634
SEG = 256
HALF = 128
HEADS = 8
DIM = 128
ROWS = HEADS * SEG
FACTOR = DIM**-0.5


def dot_nt(a, b):
    return lax.dot_general(a, b, (((1,), (1,)), ((), ())), preferred_element_type=jnp.float32)


def dot_nn(a, b):
    return lax.dot_general(a, b, (((1,), (0,)), ((), ())), preferred_element_type=jnp.float32)


def kernel(
    ctx_count,
    pair_hbm, q_hbm, k_hbm, v_hbm, o_hbm, g_hbm, lse_hbm,
    dq_ref, dk_ref, dv_ref,
    pair_ref, k_ref, v_ref, lse_ref, q_in, g_in, o_in,
    q_t, g_t, lse_b, delta_b,
    k1, k2, k3, v1, v2, v3,
    probs, dsc,
    dq_acc, own_v, own_k, sent_v, sent_k, got_v, got_k,
    in_sem, small_sem, ready,
    k_send, k_recv, v_send, v_recv, gv_send, gv_recv, gk_send, gk_recv,
):
    me = lax.axis_index("ctx")
    right = lax.rem(me + 1, ctx_count)
    left = lax.rem(me + ctx_count - 1, ctx_count)

    barrier = pltpu.get_barrier_semaphore()
    pl.semaphore_signal(barrier, inc=1, device_id={"ctx": left}, device_id_type=MESH)

    loads = []
    for i, (src, dst) in enumerate(((q_hbm, q_in), (g_hbm, g_in), (o_hbm, o_in))):
        for sg in range(2):
            load = pltpu.make_async_copy(src.at[pl.ds(sg * SEG, SEG)], dst.at[sg], in_sem.at[i, sg])
            load.start()
            loads.append(load)
    for i, (src, dst) in enumerate(((pair_hbm, pair_ref), (k_hbm, k_ref), (v_hbm, v_ref), (lse_hbm, lse_ref))):
        load = pltpu.make_async_copy(src, dst, small_sem.at[i])
        load.start()
        loads.append(load)

    keys = [None, k1, k2, k3]
    values = [None, v1, v2, v3]

    def forward(bufs, first, step, seg, send, recv):
        src = first if step == 0 else bufs[step]
        return pltpu.make_async_remote_copy(
            src_ref=src.at[:, seg],
            dst_ref=bufs[step + 1].at[:, seg],
            send_sem=send.at[step, seg],
            recv_sem=recv.at[step, seg],
            device_id={"ctx": right},
            device_id_type=MESH,
        )

    key_copy = [[forward(keys, k_hbm, s, g, k_send, k_recv) for g in range(2)] for s in range(3)]
    value_copy = [[forward(values, v_hbm, s, g, v_send, v_recv) for g in range(2)] for s in range(3)]

    def back(sent, got, step, seg, send, recv):
        return pltpu.make_async_remote_copy(
            src_ref=sent.at[step - 1, seg],
            dst_ref=got.at[step - 1, seg],
            send_sem=send.at[step - 1, seg],
            recv_sem=recv.at[step - 1, seg],
            device_id={"ctx": left},
            device_id_type=MESH,
        )

    gv_copy = [None] + [[back(sent_v, got_v, s, g, gv_send, gv_recv) for g in range(2)] for s in (1, 2, 3)]
    gk_copy = [None] + [[back(sent_k, got_k, s, g, gk_send, gk_recv) for g in range(2)] for s in (1, 2, 3)]

    pl.semaphore_wait(barrier, 1)

    def prologue():
        for load in loads:
            load.wait()
        for h in range(HEADS):
            cols = slice(h * DIM, (h + 1) * DIM)
            for sg in range(2):
                qh = q_in[sg, :, cols]
                gh = g_in[sg, :, cols]
                q_t[sg, :, h * SEG : (h + 1) * SEG] = qh.T
                g_t[sg, :, h * SEG : (h + 1) * SEG] = gh.T
                delta = jnp.sum(
                    gh.astype(jnp.float32) * o_in[sg, :, cols].astype(jnp.float32), axis=1, keepdims=True
                )
                delta_b[sg, h * SEG : (h + 1) * SEG, :] = jnp.broadcast_to(delta, (SEG, DIM))
                for j in range(SEG // DIM):
                    at = sg * SEG + j * DIM
                    row = lse_ref[h : h + 1, at : at + DIM] * LOG2E
                    lse_b[sg, h * SEG + j * DIM : h * SEG + (j + 1) * DIM, :] = jnp.broadcast_to(row, (DIM, DIM)).T
        dq_acc[...] = jnp.zeros_like(dq_acc)

    def wide(x, width):
        return jnp.concatenate([x] * (width // DIM), axis=1)

    def probs_of(q_seg, key, out, diagonal):
        width = key.shape[0]
        for h in range(HEADS):
            rows = pl.ds(h * SEG, SEG)
            x = dot_nt(q_heads(q_seg, h), key) * (FACTOR * LOG2E) - wide(lse_b[q_seg, rows, :], width)
            p = jnp.exp2(x)
            if diagonal:
                below = lax.broadcasted_iota(jnp.int32, (SEG, SEG), 1) <= lax.broadcasted_iota(
                    jnp.int32, (SEG, SEG), 0
                )
                p = jnp.where(below, p, 0.0)
            out[rows, :] = p.astype(jnp.bfloat16)

    def dscores_of(q_seg, value, pin, out):
        for h in range(HEADS):
            rows = pl.ds(h * SEG, SEG)
            dp = dot_nt(g_heads(q_seg, h), value)
            ds = pin[rows, :].astype(jnp.float32) * (dp - wide(delta_b[q_seg, rows, :], value.shape[0]))
            out[rows, :] = ds.astype(jnp.bfloat16)

    def q_heads(q_seg, h):
        return q_in[q_seg, :, h * DIM : (h + 1) * DIM]

    def g_heads(q_seg, h):
        return g_in[q_seg, :, h * DIM : (h + 1) * DIM]

    def segment(ref, seg, part=None):
        return ref[seg].reshape(SEG, DIM) if part is None else ref[seg, part]

    def add_own(own, seg, total, first):
        for part in range(2):
            cols = total[:, part * HALF : (part + 1) * HALF]
            own[0, part, seg] = cols if first else own[0, part, seg] + cols

    def own_probs(q_seg, k_seg, diagonal):
        probs_of(q_seg, segment(k_ref, k_seg), probs.at[0, 0], diagonal)

    def own_rest(q_seg, k_seg, first_k):
        p, d = probs.at[0, 0], dsc.at[0]
        dscores_of(q_seg, segment(v_ref, k_seg), p, d)
        add_own(own_v, k_seg, dot_nn(g_t[q_seg], p[...]), first_k)
        add_own(own_k, k_seg, dot_nn(q_t[q_seg], d[...]), first_k)
        dq_acc[q_seg] += dot_nn(d[...], segment(k_ref, k_seg))

    def pick(step, earlier, later):
        return jnp.where(jnp.broadcast_to(b_seg[step], earlier.shape) == 0, earlier, later)

    def spread(own, step, part, part_a, part_b):
        zero = jnp.zeros_like(part_b)
        early = part_a + pick(step, part_b, zero)
        late = pick(step, zero, part_b)
        for p in (0, 1) if part is None else (part,):
            cols = slice(p * HALF, (p + 1) * HALF) if part is None else slice(0, HALF)
            own[step, p, 0] = early[:, cols]
            own[step, p, 1] = late[:, cols]

    def columns(part):
        return slice(None) if part is None else pl.ds(part * HALF, HALF)

    def stage_v(s, part):
        qb, at = b_seg[s], columns(part)
        key_a = segment(keys[s], 0, part)
        key_b = pick(s, key_a, segment(keys[s], 1, part))
        probs_of(1, key_a, probs.at[s, 0, :, at], False)
        probs_of(qb, key_b, probs.at[s, 1, :, at], False)
        spread(own_v, s, part, dot_nn(g_t[1], probs[s, 0, :, at]), dot_nn(g_t[qb], probs[s, 1, :, at]))

    def stage_k(s, part):
        qb, at = b_seg[s], columns(part)
        value_a = segment(values[s], 0, part)
        value_b = pick(s, value_a, segment(values[s], 1, part))
        dscores_of(1, value_a, probs.at[s, 0, :, at], dsc.at[0, :, at])
        dscores_of(qb, value_b, probs.at[s, 1, :, at], dsc.at[1, :, at])
        spread(own_k, s, part, dot_nn(q_t[1], dsc[0, :, at]), dot_nn(q_t[qb], dsc[1, :, at]))

    def queries_of(s):
        key_a = segment(keys[s], 0)
        part_b = dot_nn(dsc[1], pick(s, key_a, segment(keys[s], 1)))
        zero = jnp.zeros_like(part_b)
        dq_acc[1] += dot_nn(dsc[0], key_a) + pick(s, zero, part_b)
        dq_acc[0] += pick(s, part_b, zero)

    def scaled_queries():
        for h in range(HEADS):
            for sg in range(2):
                dq_ref[sg * SEG : (sg + 1) * SEG, h * DIM : (h + 1) * DIM] = (
                    dq_acc[sg, h * SEG : (h + 1) * SEG, :] * FACTOR
                ).astype(jnp.bfloat16)

    def pass_back(copies, own, sent, got, s, seg):
        total = own[s, seg]
        if s < 3:
            copies[s + 1][seg].wait_recv()
            total = total + got[s, seg].astype(jnp.float32)
        sent[s - 1, seg] = total.astype(jnp.bfloat16)
        copies[s][seg].start()

    def finish(copies, own, got, seg, scale, out):
        copies[1][seg].wait_recv()
        total = own[0, seg] + got[0, seg].astype(jnp.float32)
        if scale is not None:
            total = total * scale
        for half in range(2):
            at = half * SEG + seg * HALF
            out[at : at + HALF, :] = total[half].T

    def arrived(copies, step, seg):
        copies[step - 1][seg].wait_recv()
        if step < 3:
            copies[step][seg].start()

    key_copy[0][0].start()
    key_copy[0][1].start()
    value_copy[0][0].start()
    pl.semaphore_signal(ready, inc=1, device_id={"ctx": right}, device_id_type=MESH)
    prologue()
    mine = pair_ref[me]
    b_seg = [None] + [
        lax.div(pair_ref[lax.rem(me + ctx_count - s, ctx_count)] - mine + ctx_count, ctx_count) for s in (1, 2, 3)
    ]
    arrived(key_copy, 1, 0)
    arrived(key_copy, 1, 1)
    value_copy[0][1].start()
    own_probs(1, 0, False)
    own_rest(1, 0, True)
    own_probs(0, 0, True)
    arrived(key_copy, 2, 0)
    own_rest(0, 0, False)
    arrived(key_copy, 2, 1)
    arrived(value_copy, 1, 0)
    arrived(value_copy, 1, 1)
    stage_v(2, None)
    arrived(key_copy, 3, 0)
    stage_v(3, 0)
    pl.semaphore_wait(ready, 1)
    pass_back(gv_copy, own_v, sent_v, got_v, 3, 0)
    own_probs(1, 1, True)
    arrived(key_copy, 3, 1)
    stage_v(3, 1)
    pass_back(gv_copy, own_v, sent_v, got_v, 3, 1)
    arrived(value_copy, 2, 0)
    stage_v(1, None)
    arrived(value_copy, 2, 1)
    pass_back(gv_copy, own_v, sent_v, got_v, 2, 0)
    pass_back(gv_copy, own_v, sent_v, got_v, 2, 1)
    arrived(value_copy, 3, 0)
    stage_k(3, 0)
    pass_back(gk_copy, own_k, sent_k, got_k, 3, 0)
    arrived(value_copy, 3, 1)
    stage_k(3, 1)
    pass_back(gk_copy, own_k, sent_k, got_k, 3, 1)
    queries_of(3)
    pass_back(gv_copy, own_v, sent_v, got_v, 1, 0)
    stage_k(2, None)
    pass_back(gk_copy, own_k, sent_k, got_k, 2, 0)
    queries_of(2)
    pass_back(gk_copy, own_k, sent_k, got_k, 2, 1)
    own_rest(1, 1, True)
    pass_back(gv_copy, own_v, sent_v, got_v, 1, 1)
    stage_k(1, None)
    pass_back(gk_copy, own_k, sent_k, got_k, 1, 0)
    pass_back(gk_copy, own_k, sent_k, got_k, 1, 1)
    finish(gv_copy, own_v, got_v, 0, None, dv_ref)
    finish(gv_copy, own_v, got_v, 1, None, dv_ref)
    queries_of(1)
    scaled_queries()
    finish(gk_copy, own_k, got_k, 0, FACTOR, dk_ref)
    finish(gk_copy, own_k, got_k, 1, FACTOR, dk_ref)
    for copies in (key_copy, value_copy, gv_copy[1:], gk_copy[1:]):
        for pair in copies:
            for copy in pair:
                copy.wait_send()


def per_device(queries, keys, values, outputs, out_grad, log_sums, pair_of):
    ctx_count = lax.axis_size("ctx")
    bf16, f32 = jnp.bfloat16, jnp.float32
    vmem = pl.BlockSpec(memory_space=pltpu.VMEM)
    hbm = pl.BlockSpec(memory_space=pltpu.HBM)
    sems = pltpu.SemaphoreType.DMA((3, 2))

    blocks = (2, 2, HALF, DIM)
    operands = (pair_of, queries, keys.reshape(blocks), values.reshape(blocks), outputs, out_grad, log_sums)

    def body(*refs):
        kernel(ctx_count, *refs)

    grads = pl.pallas_call(
        body,
        out_shape=(
            jax.ShapeDtypeStruct(queries.shape, bf16),
            jax.ShapeDtypeStruct(keys.shape, f32),
            jax.ShapeDtypeStruct(values.shape, f32),
        ),
        in_specs=[hbm] * 7,
        out_specs=(vmem, vmem, vmem),
        scratch_shapes=[
            pltpu.SMEM(pair_of.shape, jnp.int32),
            pltpu.VMEM((2, 2, HALF, DIM), bf16),
            pltpu.VMEM((2, 2, HALF, DIM), bf16),
            pltpu.VMEM(log_sums.shape, f32),
            pltpu.VMEM((2, SEG, HEADS * DIM), bf16),
            pltpu.VMEM((2, SEG, HEADS * DIM), bf16),
            pltpu.VMEM((2, SEG, HEADS * DIM), bf16),
            pltpu.VMEM((2, DIM, ROWS), bf16),
            pltpu.VMEM((2, DIM, ROWS), bf16),
            pltpu.VMEM((2, ROWS, DIM), f32),
            pltpu.VMEM((2, ROWS, DIM), f32),
        ]
        + [pltpu.VMEM((2, 2, HALF, DIM), bf16)] * 6
        + [
            pltpu.VMEM((4, 2, ROWS, SEG), bf16),
            pltpu.VMEM((2, ROWS, SEG), bf16),
            pltpu.VMEM((2, ROWS, DIM), f32),
            pltpu.VMEM((4, 2, 2, DIM, HALF), f32),
            pltpu.VMEM((4, 2, 2, DIM, HALF), f32),
            pltpu.VMEM((3, 2, 2, DIM, HALF), bf16),
            pltpu.VMEM((3, 2, 2, DIM, HALF), bf16),
            pltpu.VMEM((3, 2, 2, DIM, HALF), bf16),
            pltpu.VMEM((3, 2, 2, DIM, HALF), bf16),
            pltpu.SemaphoreType.DMA((3, 2)),
            pltpu.SemaphoreType.DMA((4,)),
            pltpu.SemaphoreType.REGULAR,
        ]
        + [sems] * 8,
        compiler_params=pltpu.CompilerParams(
            collective_id=0, has_side_effects=True, vmem_limit_bytes=40 * 2**20
        ),
        cost_estimate=pl.CostEstimate(
            flops=6_000_000_000, bytes_accessed=5_000_000, transcendentals=4_700_000
        ),
        name="gqa_backward",
    )(*(pltpu.with_memory_space_constraint(x, pltpu.HBM) for x in operands))

    def written(dq_ref, dk_ref, dv_ref, dq_hbm, dk_hbm, dv_hbm, sem):
        copies = [
            pltpu.make_async_copy(src, dst, sem.at[i])
            for i, (src, dst) in enumerate(((dq_ref, dq_hbm), (dk_ref, dk_hbm), (dv_ref, dv_hbm)))
        ]
        for copy in copies:
            copy.start()
        for copy in copies:
            copy.wait()

    return pl.pallas_call(
        written,
        out_shape=tuple(jax.ShapeDtypeStruct(x.shape, x.dtype) for x in grads),
        in_specs=[vmem] * 3,
        out_specs=(hbm,) * 3,
        scratch_shapes=[pltpu.SemaphoreType.DMA((3,))],
        compiler_params=pltpu.CompilerParams(vmem_limit_bytes=8 * 2**20),
        name="written",
    )(*grads)


def solution(mesh):
    return jax.shard_map(
        per_device,
        mesh=mesh,
        in_specs=(
            P("ctx", "grp"),
            P("ctx", "grp"),
            P("ctx", "grp"),
            P("ctx", "grp"),
            P("ctx", "grp"),
            P("grp", "ctx"),
            P(),
        ),
        out_specs=(P("ctx", "grp"), P("ctx", "grp"), P("ctx", "grp")),
        check_vma=False,
    )
```

```python
import jax
import jax.numpy as jnp
from jax import lax
from jax.experimental import pallas as pl
from jax.experimental.pallas import tpu as pltpu
from jax.sharding import PartitionSpec as P

MESH = pl.DeviceIdType.MESH
LOG2E = 1.4426950408889634
SEG = 256
HALF = 128
HEADS = 8
DIM = 128
ROWS = HEADS * SEG
FACTOR = DIM**-0.5


def dot_nt(a, b):
    return lax.dot_general(a, b, (((1,), (1,)), ((), ())), preferred_element_type=jnp.float32)


def dot_nn(a, b):
    return lax.dot_general(a, b, (((1,), (0,)), ((), ())), preferred_element_type=jnp.float32)


def kernel(
    ctx_count,
    pair_hbm, q_hbm, k_hbm, v_hbm, o_hbm, g_hbm, lse_hbm,
    dq_ref, dk_ref, dv_ref,
    pair_ref, k_ref, v_ref, lse_ref, q_in, g_in, o_in,
    q_t, g_t, lse_b, delta_b,
    k1, k2, k3, v1, v2, v3,
    probs, dsc,
    dq_acc, own_v, own_k, sent_v, sent_k, got_v, got_k,
    in_sem, small_sem, ready,
    k_send, k_recv, v_send, v_recv, gv_send, gv_recv, gk_send, gk_recv,
):
    me = lax.axis_index("ctx")
    right = lax.rem(me + 1, ctx_count)
    left = lax.rem(me + ctx_count - 1, ctx_count)

    barrier = pltpu.get_barrier_semaphore()
    pl.semaphore_signal(barrier, inc=1, device_id={"ctx": left}, device_id_type=MESH)

    loads = []
    for i, (src, dst) in enumerate(((q_hbm, q_in), (g_hbm, g_in), (o_hbm, o_in))):
        for sg in range(2):
            load = pltpu.make_async_copy(src.at[pl.ds(sg * SEG, SEG)], dst.at[sg], in_sem.at[i, sg])
            load.start()
            loads.append(load)
    for i, (src, dst) in enumerate(((pair_hbm, pair_ref), (k_hbm, k_ref), (v_hbm, v_ref), (lse_hbm, lse_ref))):
        load = pltpu.make_async_copy(src, dst, small_sem.at[i])
        load.start()
        loads.append(load)

    keys = [None, k1, k2, k3]
    values = [None, v1, v2, v3]

    def forward(bufs, first, step, seg, send, recv):
        src = first if step == 0 else bufs[step]
        return pltpu.make_async_remote_copy(
            src_ref=src.at[:, seg],
            dst_ref=bufs[step + 1].at[:, seg],
            send_sem=send.at[step, seg],
            recv_sem=recv.at[step, seg],
            device_id={"ctx": right},
            device_id_type=MESH,
        )

    key_copy = [[forward(keys, k_hbm, s, g, k_send, k_recv) for g in range(2)] for s in range(3)]
    value_copy = [[forward(values, v_hbm, s, g, v_send, v_recv) for g in range(2)] for s in range(3)]

    def back(sent, got, step, seg, send, recv):
        return pltpu.make_async_remote_copy(
            src_ref=sent.at[step - 1, seg],
            dst_ref=got.at[step - 1, seg],
            send_sem=send.at[step - 1, seg],
            recv_sem=recv.at[step - 1, seg],
            device_id={"ctx": left},
            device_id_type=MESH,
        )

    gv_copy = [None] + [[back(sent_v, got_v, s, g, gv_send, gv_recv) for g in range(2)] for s in (1, 2, 3)]
    gk_copy = [None] + [[back(sent_k, got_k, s, g, gk_send, gk_recv) for g in range(2)] for s in (1, 2, 3)]

    pl.semaphore_wait(barrier, 1)

    def prologue():
        for load in loads:
            load.wait()
        for h in range(HEADS):
            cols = slice(h * DIM, (h + 1) * DIM)
            for sg in range(2):
                qh = q_in[sg, :, cols]
                gh = g_in[sg, :, cols]
                q_t[sg, :, h * SEG : (h + 1) * SEG] = qh.T
                g_t[sg, :, h * SEG : (h + 1) * SEG] = gh.T
                delta = jnp.sum(
                    gh.astype(jnp.float32) * o_in[sg, :, cols].astype(jnp.float32), axis=1, keepdims=True
                )
                delta_b[sg, h * SEG : (h + 1) * SEG, :] = jnp.broadcast_to(delta, (SEG, DIM))
                for j in range(SEG // DIM):
                    at = sg * SEG + j * DIM
                    row = lse_ref[h : h + 1, at : at + DIM] * LOG2E
                    lse_b[sg, h * SEG + j * DIM : h * SEG + (j + 1) * DIM, :] = jnp.broadcast_to(row, (DIM, DIM)).T
        dq_acc[...] = jnp.zeros_like(dq_acc)

    def wide(x, width):
        return jnp.concatenate([x] * (width // DIM), axis=1)

    def probs_of(q_seg, key, out, diagonal):
        width = key.shape[0]
        for h in range(HEADS):
            rows = pl.ds(h * SEG, SEG)
            x = dot_nt(q_heads(q_seg, h), key) * (FACTOR * LOG2E) - wide(lse_b[q_seg, rows, :], width)
            p = jnp.exp2(x)
            if diagonal:
                below = lax.broadcasted_iota(jnp.int32, (SEG, SEG), 1) <= lax.broadcasted_iota(
                    jnp.int32, (SEG, SEG), 0
                )
                p = jnp.where(below, p, 0.0)
            out[rows, :] = p.astype(jnp.bfloat16)

    def dscores_of(q_seg, value, pin, out):
        for h in range(HEADS):
            rows = pl.ds(h * SEG, SEG)
            dp = dot_nt(g_heads(q_seg, h), value)
            ds = pin[rows, :].astype(jnp.float32) * (dp - wide(delta_b[q_seg, rows, :], value.shape[0]))
            out[rows, :] = ds.astype(jnp.bfloat16)

    def q_heads(q_seg, h):
        return q_in[q_seg, :, h * DIM : (h + 1) * DIM]

    def g_heads(q_seg, h):
        return g_in[q_seg, :, h * DIM : (h + 1) * DIM]

    def segment(ref, seg, part=None):
        return ref[seg].reshape(SEG, DIM) if part is None else ref[seg, part]

    def add_own(own, seg, total, first):
        for part in range(2):
            cols = total[:, part * HALF : (part + 1) * HALF]
            own[0, part, seg] = cols if first else own[0, part, seg] + cols

    def own_probs(q_seg, k_seg, diagonal):
        probs_of(q_seg, segment(k_ref, k_seg), probs.at[0, 0], diagonal)

    def own_rest(q_seg, k_seg, first_k):
        p, d = probs.at[0, 0], dsc.at[0]
        dscores_of(q_seg, segment(v_ref, k_seg), p, d)
        add_own(own_v, k_seg, dot_nn(g_t[q_seg], p[...]), first_k)
        add_own(own_k, k_seg, dot_nn(q_t[q_seg], d[...]), first_k)
        dq_acc[q_seg] += dot_nn(d[...], segment(k_ref, k_seg))

    def pick(step, earlier, later):
        return jnp.where(jnp.broadcast_to(b_seg[step], earlier.shape) == 0, earlier, later)

    def spread(own, step, part, part_a, part_b):
        zero = jnp.zeros_like(part_b)
        early = part_a + pick(step, part_b, zero)
        late = pick(step, zero, part_b)
        for p in (0, 1) if part is None else (part,):
            cols = slice(p * HALF, (p + 1) * HALF) if part is None else slice(0, HALF)
            own[step, p, 0] = early[:, cols]
            own[step, p, 1] = late[:, cols]

    def columns(part):
        return slice(None) if part is None else pl.ds(part * HALF, HALF)

    def stage_v(s, part):
        qb, at = b_seg[s], columns(part)
        key_a = segment(keys[s], 0, part)
        key_b = pick(s, key_a, segment(keys[s], 1, part))
        probs_of(1, key_a, probs.at[s, 0, :, at], False)
        probs_of(qb, key_b, probs.at[s, 1, :, at], False)
        spread(own_v, s, part, dot_nn(g_t[1], probs[s, 0, :, at]), dot_nn(g_t[qb], probs[s, 1, :, at]))

    def stage_k(s, part):
        qb, at = b_seg[s], columns(part)
        value_a = segment(values[s], 0, part)
        value_b = pick(s, value_a, segment(values[s], 1, part))
        dscores_of(1, value_a, probs.at[s, 0, :, at], dsc.at[0, :, at])
        dscores_of(qb, value_b, probs.at[s, 1, :, at], dsc.at[1, :, at])
        spread(own_k, s, part, dot_nn(q_t[1], dsc[0, :, at]), dot_nn(q_t[qb], dsc[1, :, at]))

    def queries_of(s):
        key_a = segment(keys[s], 0)
        part_b = dot_nn(dsc[1], pick(s, key_a, segment(keys[s], 1)))
        zero = jnp.zeros_like(part_b)
        dq_acc[1] += dot_nn(dsc[0], key_a) + pick(s, zero, part_b)
        dq_acc[0] += pick(s, part_b, zero)

    def scaled_queries():
        for h in range(HEADS):
            for sg in range(2):
                dq_ref[sg * SEG : (sg + 1) * SEG, h * DIM : (h + 1) * DIM] = (
                    dq_acc[sg, h * SEG : (h + 1) * SEG, :] * FACTOR
                ).astype(jnp.bfloat16)

    def pass_back(copies, own, sent, got, s, seg):
        total = own[s, seg]
        if s < 3:
            copies[s + 1][seg].wait_recv()
            total = total + got[s, seg].astype(jnp.float32)
        sent[s - 1, seg] = total.astype(jnp.bfloat16)
        copies[s][seg].start()

    def finish(copies, own, got, seg, scale, out):
        copies[1][seg].wait_recv()
        total = own[0, seg] + got[0, seg].astype(jnp.float32)
        if scale is not None:
            total = total * scale
        for half in range(2):
            at = half * SEG + seg * HALF
            out[at : at + HALF, :] = total[half].T

    def arrived(copies, step, seg):
        copies[step - 1][seg].wait_recv()
        if step < 3:
            copies[step][seg].start()

    key_copy[0][0].start()
    key_copy[0][1].start()
    value_copy[0][0].start()
    pl.semaphore_signal(ready, inc=1, device_id={"ctx": right}, device_id_type=MESH)
    prologue()
    mine = pair_ref[me]
    b_seg = [None] + [
        lax.div(pair_ref[lax.rem(me + ctx_count - s, ctx_count)] - mine + ctx_count, ctx_count) for s in (1, 2, 3)
    ]
    arrived(key_copy, 1, 0)
    arrived(key_copy, 1, 1)
    value_copy[0][1].start()
    own_probs(1, 0, False)
    own_rest(1, 0, True)
    own_probs(0, 0, True)
    arrived(key_copy, 2, 0)
    own_rest(0, 0, False)
    arrived(key_copy, 2, 1)
    arrived(value_copy, 1, 0)
    arrived(value_copy, 1, 1)
    stage_v(2, None)
    arrived(key_copy, 3, 0)
    stage_v(3, 0)
    pl.semaphore_wait(ready, 1)
    pass_back(gv_copy, own_v, sent_v, got_v, 3, 0)
    arrived(key_copy, 3, 1)
    stage_v(3, 1)
    pass_back(gv_copy, own_v, sent_v, got_v, 3, 1)
    arrived(value_copy, 2, 0)
    stage_v(1, None)
    arrived(value_copy, 2, 1)
    pass_back(gv_copy, own_v, sent_v, got_v, 2, 0)
    pass_back(gv_copy, own_v, sent_v, got_v, 2, 1)
    own_probs(1, 1, True)
    arrived(value_copy, 3, 0)
    stage_k(3, 0)
    pass_back(gk_copy, own_k, sent_k, got_k, 3, 0)
    arrived(value_copy, 3, 1)
    stage_k(3, 1)
    pass_back(gk_copy, own_k, sent_k, got_k, 3, 1)
    pass_back(gv_copy, own_v, sent_v, got_v, 1, 0)
    queries_of(3)
    stage_k(2, None)
    pass_back(gk_copy, own_k, sent_k, got_k, 2, 0)
    queries_of(2)
    pass_back(gk_copy, own_k, sent_k, got_k, 2, 1)
    pass_back(gv_copy, own_v, sent_v, got_v, 1, 1)
    own_rest(1, 1, True)
    stage_k(1, None)
    pass_back(gk_copy, own_k, sent_k, got_k, 1, 0)
    pass_back(gk_copy, own_k, sent_k, got_k, 1, 1)
    queries_of(1)
    finish(gv_copy, own_v, got_v, 0, None, dv_ref)
    finish(gv_copy, own_v, got_v, 1, None, dv_ref)
    scaled_queries()
    finish(gk_copy, own_k, got_k, 0, FACTOR, dk_ref)
    finish(gk_copy, own_k, got_k, 1, FACTOR, dk_ref)
    for copies in (key_copy, value_copy, gv_copy[1:], gk_copy[1:]):
        for pair in copies:
            for copy in pair:
                copy.wait_send()


def per_device(queries, keys, values, outputs, out_grad, log_sums, pair_of):
    ctx_count = lax.axis_size("ctx")
    bf16, f32 = jnp.bfloat16, jnp.float32
    vmem = pl.BlockSpec(memory_space=pltpu.VMEM)
    hbm = pl.BlockSpec(memory_space=pltpu.HBM)
    sems = pltpu.SemaphoreType.DMA((3, 2))

    blocks = (2, 2, HALF, DIM)
    operands = (pair_of, queries, keys.reshape(blocks), values.reshape(blocks), outputs, out_grad, log_sums)

    def body(*refs):
        kernel(ctx_count, *refs)

    grads = pl.pallas_call(
        body,
        out_shape=(
            jax.ShapeDtypeStruct(queries.shape, bf16),
            jax.ShapeDtypeStruct(keys.shape, f32),
            jax.ShapeDtypeStruct(values.shape, f32),
        ),
        in_specs=[hbm] * 7,
        out_specs=(vmem, vmem, vmem),
        scratch_shapes=[
            pltpu.SMEM(pair_of.shape, jnp.int32),
            pltpu.VMEM((2, 2, HALF, DIM), bf16),
            pltpu.VMEM((2, 2, HALF, DIM), bf16),
            pltpu.VMEM(log_sums.shape, f32),
            pltpu.VMEM((2, SEG, HEADS * DIM), bf16),
            pltpu.VMEM((2, SEG, HEADS * DIM), bf16),
            pltpu.VMEM((2, SEG, HEADS * DIM), bf16),
            pltpu.VMEM((2, DIM, ROWS), bf16),
            pltpu.VMEM((2, DIM, ROWS), bf16),
            pltpu.VMEM((2, ROWS, DIM), f32),
            pltpu.VMEM((2, ROWS, DIM), f32),
        ]
        + [pltpu.VMEM((2, 2, HALF, DIM), bf16)] * 6
        + [
            pltpu.VMEM((4, 2, ROWS, SEG), bf16),
            pltpu.VMEM((2, ROWS, SEG), bf16),
            pltpu.VMEM((2, ROWS, DIM), f32),
            pltpu.VMEM((4, 2, 2, DIM, HALF), f32),
            pltpu.VMEM((4, 2, 2, DIM, HALF), f32),
            pltpu.VMEM((3, 2, 2, DIM, HALF), bf16),
            pltpu.VMEM((3, 2, 2, DIM, HALF), bf16),
            pltpu.VMEM((3, 2, 2, DIM, HALF), bf16),
            pltpu.VMEM((3, 2, 2, DIM, HALF), bf16),
            pltpu.SemaphoreType.DMA((3, 2)),
            pltpu.SemaphoreType.DMA((4,)),
            pltpu.SemaphoreType.REGULAR,
        ]
        + [sems] * 8,
        compiler_params=pltpu.CompilerParams(
            collective_id=0, has_side_effects=True, vmem_limit_bytes=40 * 2**20
        ),
        cost_estimate=pl.CostEstimate(
            flops=6_000_000_000, bytes_accessed=5_000_000, transcendentals=4_700_000
        ),
        name="gqa_backward",
    )(*(pltpu.with_memory_space_constraint(x, pltpu.HBM) for x in operands))

    def written(dq_ref, dk_ref, dv_ref, dq_hbm, dk_hbm, dv_hbm, sem):
        copies = [
            pltpu.make_async_copy(src, dst, sem.at[i])
            for i, (src, dst) in enumerate(((dq_ref, dq_hbm), (dk_ref, dk_hbm), (dv_ref, dv_hbm)))
        ]
        for copy in copies:
            copy.start()
        for copy in copies:
            copy.wait()

    return pl.pallas_call(
        written,
        out_shape=tuple(jax.ShapeDtypeStruct(x.shape, x.dtype) for x in grads),
        in_specs=[vmem] * 3,
        out_specs=(hbm,) * 3,
        scratch_shapes=[pltpu.SemaphoreType.DMA((3,))],
        compiler_params=pltpu.CompilerParams(vmem_limit_bytes=8 * 2**20),
        name="written",
    )(*grads)


def solution(mesh):
    return jax.shard_map(
        per_device,
        mesh=mesh,
        in_specs=(
            P("ctx", "grp"),
            P("ctx", "grp"),
            P("ctx", "grp"),
            P("ctx", "grp"),
            P("ctx", "grp"),
            P("grp", "ctx"),
            P(),
        ),
        out_specs=(P("ctx", "grp"), P("ctx", "grp"), P("ctx", "grp")),
        check_vma=False,
    )
```
